256 devices in a mesh: blk: 128 (over y, x_hi, z, core), col: 2 (over x_lo).
Axes of the slice: x: 4 (x_hi: 2, x_lo: 2; x = x_hi * 2 + x_lo), y: 4, z: 8, core: 2. Of those that a mesh axis runs over, the one named last changes fastest.
Arguments:
- features: bfloat16 [131072, 256], P('blk', 'col'), may hold values from -6 to 6
- tile_values: bfloat16 [36864, 128, 128], P('blk'), may hold values from -0.09375 to 0.09375
- tile_index: int32 [3, 36864], P(None, 'blk'), may hold values from 0 to 127, as said below
- send_rows: int32 [128, 128, 8], P('blk'), may hold values from 0 to 1023
- slot_counts: int32 [128, 128], P('blk'), may hold values from 0 to 8, as said below
- far_weight: bfloat16 [131072, 1024], P('blk'), may hold values from -0.1875 to 0.1875
- weight_one: bfloat16 [256, 256], replicated, may hold values from -0.375 to 0.375
- weight_two: bfloat16 [256, 256], replicated, may hold values from -0.375 to 0.375
Outputs:
- node_output: bfloat16 [131072, 256], P('blk', 'col')
The draws below stay inside these ranges and needn't reach their ends.
Inputs may be any that keep to these rules, and one draw needn't show every extreme that they name: tile_index[0, t] is a partition at most 4 steps from t // 288 around the closed cycle of 128 partitions, and every cycle offset from -4 to 4 occurs among each partition's tiles; tile_index[1, t] and tile_index[2, t] are row tiles below 8; tiles may repeat. `slot_counts`: some partition receives 8 live slots from every partition.
All inputs are finite; a program needn't handle non-finite values.
Results may differ from the reference program's by a relative error of at most 0.008.
Values may be sent and summed in bfloat16 or wider, within the bound.
A program may use at most 64 MiB of HBM per device.

```python
import jax
import jax.numpy as jnp
from jax import lax

F = 256
TILE = 128
REACH = 4
TPR = 36
CAP = 8
RT = 8
ROWS = 1024
NT = 288
TILES = 36864
NODES = 131072
SLOTS = 1024
N_BLK = 128


def draw_tile_index(key, part):
    key = jax.random.fold_in(key, 11)
    first_key, second_key, third_key, fourth_key = jax.random.split(key, 4)
    partitions = TILES // NT
    spread = jax.random.randint(first_key, (partitions, NT), -REACH, REACH + 1)
    position = jnp.arange(NT, dtype=jnp.int32)[None, :]
    base = jnp.where(position < 2 * REACH + 1, position - REACH, spread)
    scores = jax.random.randint(second_key, (partitions, NT), 0, 2 ** 20) * NT + position
    order = jnp.argsort(scores, axis=1, stable=True)
    offsets = jnp.take_along_axis(base, order, axis=1)
    owner = jnp.arange(partitions, dtype=jnp.int32)[:, None]
    source = (owner + offsets) % partitions
    source_tile = jax.random.randint(third_key, (partitions, NT), 0, RT)
    target_tile = jax.random.randint(fourth_key, (partitions, NT), 0, RT)
    return jnp.stack([source.reshape(-1), source_tile.reshape(-1), target_tile.reshape(-1)]).astype(jnp.int32)


def draw_slot_counts(key, part):
    key = jax.random.fold_in(key, 12)
    first_key, second_key = jax.random.split(key, 2)
    partitions = NODES // ROWS
    base = jax.random.randint(first_key, (partitions, partitions), 0, CAP + 1)
    busiest = jax.random.randint(second_key, (), 0, partitions)
    column = jnp.arange(partitions, dtype=jnp.int32)[None, :]
    return jnp.where(column == busiest, CAP, base).astype(jnp.int32)


def with_ends(values, stream_key, least, largest):
    spot = [jax.random.randint(jax.random.fold_in(stream_key, axis), (), 0, length) for axis, length in enumerate(values.shape)]
    widest = values.shape.index(max(values.shape))
    neighbour = spot[:widest] + [(spot[widest] + 1) % values.shape[widest]] + spot[widest + 1:]
    return values.at[tuple(spot)].set(least).at[tuple(neighbour)].set(largest)


def shard_levels(rng, dims, pieces, smallest, largest):
    loudness = 1.0
    for dim, blocks in pieces:
        steps = jax.random.uniform(jax.random.fold_in(jax.random.fold_in(rng, 6), dim), (blocks,), jnp.float32, smallest / len(pieces), largest / len(pieces))
        loudness = loudness * jnp.repeat(jnp.exp(steps), dims[dim] // blocks).reshape((-1,) + (1,) * (len(dims) - 1 - dim))
    return loudness


def scatter_about(own_key, extent, scale, bound, pieces=(), kind=jnp.bfloat16):
    values = jax.random.normal(own_key, extent, jnp.float32) * scale
    if len(pieces) > 0:
        values = shard_levels(own_key, extent, pieces, -0.22, 0.18) * values
    return jnp.clip(values, min=-bound, max=bound).astype(kind)


def setup_inputs(seed: int = 0) -> dict:
    splits = jax.random.split(jax.random.key(seed), 9)
    features = scatter_about(splits[0], (NODES, F), 1.0, 6.0, ((0, 128), (1, 2)))
    tile_values = scatter_about(splits[1], (TILES, TILE, TILE), (TPR * TILE) ** -0.5, 0.09375, ((0, 128),))
    tile_index = draw_tile_index(jax.random.fold_in(splits[8], 71), 0)
    send_rows = with_ends(jax.random.randint(splits[3], (N_BLK, N_BLK, CAP), 0, ROWS), jax.random.fold_in(splits[3], 1), 0, ROWS - 1).astype(jnp.int32)
    slot_counts = draw_slot_counts(jax.random.fold_in(splits[8], 71), 0)
    far_weight = scatter_about(splits[5], (NODES, SLOTS), SLOTS ** -0.5, 0.1875, ((0, 128),))
    weight_one = scatter_about(splits[6], (F, F), F ** -0.5, 0.375)
    weight_two = scatter_about(splits[7], (F, F), F ** -0.5, 0.375)
    return dict(features=features, tile_values=tile_values, tile_index=tile_index, send_rows=send_rows, slot_counts=slot_counts, far_weight=far_weight, weight_one=weight_one, weight_two=weight_two)


def aggregate(field, tile_values, tile_index, send_rows, slot_counts, far_weight):
    field_tiles = field.reshape(N_BLK * RT, TILE, F)
    field_parts = field.reshape(N_BLK, ROWS, F)
    gathered = jax.vmap(lambda part_rows, index_rows: part_rows[index_rows])(field_parts, send_rows)
    live_slots = (jnp.arange(CAP, dtype=jnp.int32)[None, None, :] < slot_counts[:, :, None])
    gathered = jnp.where(live_slots[..., None], gathered, jnp.zeros_like(gathered))
    arrived = jnp.transpose(gathered, (1, 0, 2, 3)).reshape(N_BLK, SLOTS, F)
    source_tiles = (tile_index[0] * RT + tile_index[1]).astype(jnp.int32).reshape(N_BLK, NT)
    target_tiles = tile_index[2].astype(jnp.int32).reshape(N_BLK, NT)
    values_parts = tile_values.reshape(N_BLK, NT, TILE, TILE)
    weight_parts = far_weight.reshape(N_BLK, ROWS, SLOTS)

    def partition_term(packed):
        values_part, source_part, target_part, weight_part, arrived_part = packed
        sources = field_tiles[source_part].astype(jnp.float32)
        products = jnp.einsum("tij,tjc->tic", values_part.astype(jnp.float32), sources)
        near_term = jax.ops.segment_sum(products, target_part, num_segments=RT).reshape(ROWS, F)
        far_term = jnp.dot(weight_part, arrived_part, preferred_element_type=jnp.float32)
        return (near_term + far_term).astype(jnp.bfloat16)

    result = lax.map(partition_term, (values_parts, source_tiles, target_tiles, weight_parts, arrived))
    return result.reshape(NODES, F)


def reference(features, tile_values, tile_index, send_rows, slot_counts, far_weight, weight_one, weight_two):
    first = aggregate(features, tile_values, tile_index, send_rows, slot_counts, far_weight)
    hidden = jnp.maximum(jnp.dot(first, weight_one, preferred_element_type=jnp.float32), 0.0).astype(jnp.bfloat16)
    second = aggregate(hidden, tile_values, tile_index, send_rows, slot_counts, far_weight)
    return jnp.dot(second, weight_two, preferred_element_type=jnp.float32).astype(jnp.bfloat16)
```

```python
import functools

import jax
import jax.numpy as jnp
from jax import lax
from jax.experimental import pallas as pl
from jax.experimental.pallas import tpu as pltpu
from jax.sharding import PartitionSpec as P

MESH = pl.DeviceIdType.MESH
BF16 = jnp.bfloat16
F32 = jnp.float32
TILE = 128
REACH = 4
SLOTS_NEAR = 2 * REACH + 1
ROW_TILES = 8
ROWS = 1024
WIDTH = 128
CHUNKS = 4
CHUNK = ROWS // CHUNKS
RING = 16
GROUPS = 8
EMPTY = 288


def dot(a, b):
    return jnp.dot(a, b, preferred_element_type=F32)


def kernel(
    blocks, table_ref, earlier_ref, lists_ref, x_hbm, tiles_hbm, far_hbm, w1_hbm, w2_hbm, out_ref,
    tiles, sums, far, w1, w2, field, total, pair, picks, outgoing, middle, sorted_out, landed, arrived,
    load_sem, near_send, near_recv, group_send, group_recv, ring_send, ring_recv, col_send, col_recv,
):
    blk = lax.axis_index("blk")
    col = lax.axis_index("col")
    core = lax.rem(blk, 2)
    up = lax.rem(blk + 2, blocks)
    down = lax.rem(blk + blocks - 2, blocks)
    sibling = blk + 1 - 2 * core
    place = lax.rem(blk, RING)
    ring_base = blk - place
    group = blk // RING

    x_load = pltpu.make_async_copy(x_hbm, field.at[0, 4], load_sem.at[0])
    tiles_load = pltpu.make_async_copy(tiles_hbm, tiles.at[pl.ds(0, EMPTY)], load_sem.at[1])
    w1_load = pltpu.make_async_copy(w1_hbm, w1, load_sem.at[2])
    w2_load = pltpu.make_async_copy(w2_hbm, w2, load_sem.at[3])
    far_load = pltpu.make_async_copy(far_hbm, far, load_sem.at[4])
    x_load.start()
    tiles_load.start()
    far_load.start()
    w1_load.start()
    w2_load.start()

    barrier = pltpu.get_barrier_semaphore()

    def greet(**device):
        pl.semaphore_signal(barrier, inc=1, device_id=device, device_id_type=MESH)

    for k in range(1, RING):
        greet(blk=ring_base + lax.rem(place + k, RING))
    for k in range(1, GROUPS):
        greet(blk=lax.rem(group + k, GROUPS) * RING + place)
    greet(blk=up)
    greet(blk=down)
    greet(col=1 - col)

    def remote(src, dst, send, recv, **device):
        return pltpu.make_async_remote_copy(
            src_ref=src, dst_ref=dst, send_sem=send, recv_sem=recv, device_id=device, device_id_type=MESH
        )

    for a in range(ROW_TILES):
        column = jnp.broadcast_to(lists_ref[a : a + 1, :], (TILE, TILE)).T
        for b in range(ROW_TILES):
            numbers = lax.broadcasted_iota(jnp.int32, (TILE, TILE), 1) + b * TILE
            picks[a * TILE : (a + 1) * TILE, b * TILE : (b + 1) * TILE] = jnp.where(
                column == numbers, 1.0, 0.0
            ).astype(BF16)

    def pick(layer):
        for a in range(CHUNKS):
            rows = dot(picks[a * CHUNK : (a + 1) * CHUNK, :], field[layer, 4])
            outgoing[layer, 2 * a : 2 * a + 2] = rows.astype(BF16).reshape(2, TILE, WIDTH)
        middle[layer, group] = outgoing[layer, group]

    def send_groups(layer):
        for k in range(1, GROUPS):
            other = lax.rem(group + k, GROUPS)
            remote(
                outgoing.at[layer, other], middle.at[layer, group],
                group_send.at[layer], group_recv.at[layer], blk=other * RING + place,
            ).start()

    def send_ring(layer):
        part = pl.ds(0, GROUPS - 1)
        remote(
            outgoing.at[layer, part], middle.at[layer, part], group_send.at[layer], group_recv.at[layer], blk=sibling
        ).wait_recv()
        rows = middle[layer].astype(F32).reshape(GROUPS, RING, 8, WIDTH)
        sorted_out[layer] = rows.transpose(1, 0, 2, 3).reshape(RING, GROUPS * 8, WIDTH).astype(BF16)
        landed[layer, place] = sorted_out[layer, place]
        for k in range(1, RING):
            other = lax.rem(place + k, RING)
            remote(
                sorted_out.at[layer, other], landed.at[layer, place],
                ring_send.at[layer], ring_recv.at[layer], blk=ring_base + other,
            ).start()

    def collect(layer):
        part = pl.ds(0, RING - 1)
        remote(
            sorted_out.at[layer, part], landed.at[layer, part], ring_send.at[layer], ring_recv.at[layer], blk=sibling
        ).wait_recv()
        rows = landed[layer].astype(F32).reshape(RING, GROUPS, 8, WIDTH)
        arrived[...] = rows.transpose(1, 0, 2, 3).reshape(ROWS, WIDTH).astype(BF16)

    def chunk(j):
        return pl.ds(pl.multiple_of(j * CHUNK, CHUNK), CHUNK)

    def send_near(layer, kind, j, source, target, device):
        remote(
            field.at[layer, source, chunk(j)], field.at[layer, target, chunk(j)],
            near_send.at[layer, kind], near_recv.at[layer, target, j], blk=device,
        ).start()

    def send_own(layer, j):
        send_near(layer, 0, j, 4, 2, up)
        send_near(layer, 1, j, 4, 6, down)
        send_near(layer, 2, j, 4, 3 + 2 * core, sibling)

    def wait_near(layer, slot, j):
        remote(
            field.at[layer, slot, chunk(j)], field.at[layer, slot, chunk(j)],
            near_send.at[layer, 0], near_recv.at[layer, slot, j], blk=sibling,
        ).wait_recv()

    def add(layer, terms, fresh=False):
        for r in range(0, ROW_TILES, 2):
            result = None if fresh else jnp.concatenate([total[r], total[r + 1]], axis=0)
            for slot, j in terms:
                values = jnp.concatenate(
                    [
                        jnp.concatenate(
                            [tiles[table_ref[slot * 64 + row * 8 + 2 * j + half]] for half in (0, 1)], axis=1
                        )
                        for row in (r, r + 1)
                    ],
                    axis=0,
                )
                product = dot(values, field[layer, slot, chunk(j)])
                result = product if result is None else result + product
            total[r] = result[:TILE]
            total[r + 1] = result[TILE:]

    own_odd, low_odd, high_odd, last_odd = 5 - 2 * core, 3 - 2 * core, 7 - 2 * core, 1 + 6 * core

    def aggregate(layer):
        add(layer, [(4, j) for j in range(CHUNKS)], fresh=True)

        def first_hop(j, carry):
            wait_near(layer, 2, j)
            send_near(layer, 3, j, 2, 0, up)
            send_near(layer, 4, j, 2, 1 + 2 * core, sibling)
            wait_near(layer, 6, j)
            send_near(layer, 5, j, 6, 8, down)
            send_near(layer, 6, j, 6, 5 + 2 * core, sibling)
            wait_near(layer, own_odd, j)
            add(layer, [(own_odd, j), (2, j), (6, j)])
            return carry

        lax.fori_loop(0, CHUNKS, first_hop, 0)
        send_ring(layer)

        def second_hop(j, carry):
            wait_near(layer, 0, j)
            wait_near(layer, 8, j)
            send_near(layer, 7, j, 8 - 8 * core, 7 - 6 * core, sibling)
            wait_near(layer, low_odd, j)
            wait_near(layer, high_odd, j)
            add(layer, [(0, j), (8, j), (low_odd, j), (high_odd, j)])
            return carry

        lax.fori_loop(0, CHUNKS, second_hop, 0)

        def last_hop(j, carry):
            wait_near(layer, last_odd, j)
            return carry

        lax.fori_loop(0, CHUNKS, last_hop, 0)
        add(layer, [(last_odd, j) for j in range(CHUNKS)])
        collect(layer)

    def finish(j):
        near = jnp.concatenate([total[2 * j], total[2 * j + 1]], axis=0)
        return (near + dot(far[chunk(j)], arrived[...])).astype(BF16)

    x_load.wait()
    pick(0)
    pl.semaphore_wait(barrier, (RING - 1) + (GROUPS - 1) + 3)
    send_groups(0)
    for j in range(CHUNKS):
        send_own(0, j)

    tiles_load.wait()
    sums[EMPTY] = jnp.zeros((TILE, TILE), F32)
    tiles[EMPTY] = jnp.zeros((TILE, TILE), BF16)

    def add_earlier(t, carry):
        value = tiles[t].astype(F32) + sums[earlier_ref[t]]
        sums[t] = value
        tiles[t] = value.astype(BF16)
        return carry

    lax.fori_loop(0, EMPTY, add_earlier, 0, unroll=2)

    aggregate(0)
    far_load.wait()

    def exchange(j):
        return remote(pair.at[col, chunk(j)], pair.at[col, chunk(j)], col_send, col_recv.at[j], col=1 - col)

    def finish_first(j, carry):
        pair[col, chunk(j)] = finish(j)
        exchange(j).start()
        return carry

    lax.fori_loop(0, CHUNKS, finish_first, 0)
    w1_load.wait()
    w2_load.wait()
    half = pl.ds(pl.multiple_of(col * WIDTH, WIDTH), WIDTH)

    def project(j, carry):
        remote(
            pair.at[1 - col, chunk(j)], pair.at[1 - col, chunk(j)], col_send, col_recv.at[j], col=1 - col
        ).wait_recv()
        both = jnp.concatenate([pair[0, chunk(j)], pair[1, chunk(j)]], axis=1)
        hidden = jnp.maximum(dot(both, w1[...]), 0.0).astype(BF16)
        field[1, 4, chunk(j)] = dot(hidden, w2[:, half]).astype(BF16)
        send_own(1, j)
        return carry

    lax.fori_loop(0, CHUNKS, project, 0)
    pick(1)
    send_groups(1)
    aggregate(1)

    def finish_second(j, carry):
        out_ref[chunk(j)] = finish(j)
        return carry

    lax.fori_loop(0, CHUNKS, finish_second, 0)

    for layer in range(2):
        for kind in range(8):
            remote(
                field.at[layer, 4], field.at[layer, 4], near_send.at[layer, kind], near_recv.at[layer, 4, 0], blk=sibling
            ).wait_send()
        part = pl.ds(0, GROUPS - 1)
        remote(
            outgoing.at[layer, part], middle.at[layer, part], group_send.at[layer], group_recv.at[layer], blk=sibling
        ).wait_send()
        part = pl.ds(0, RING - 1)
        remote(
            sorted_out.at[layer, part], landed.at[layer, part], ring_send.at[layer], ring_recv.at[layer], blk=sibling
        ).wait_send()
    remote(pair.at[0], pair.at[0], col_send, col_recv.at[0], col=1 - col).wait_send()


def body(
    features, tile_values, tile_index, send_rows, slot_counts, far_weight, weight_one, weight_two
):
    blocks = lax.axis_size("blk")
    position = lax.axis_index("blk")
    capacity = send_rows.shape[2]
    tile_count = tile_values.shape[0]
    offset = (tile_index[0] - position + REACH + blocks) % blocks
    key = offset * 64 + tile_index[2] * ROW_TILES + tile_index[1]
    numbers = jnp.arange(tile_count, dtype=jnp.int32)
    same = (key[:, None] == key[None, :]) & (numbers[:, None] < numbers[None, :])
    earlier = jnp.max(jnp.where(same, numbers[:, None], -1), axis=0)
    earlier = jnp.where(earlier < 0, EMPTY, earlier)
    entries = jnp.arange(SLOTS_NEAR * 64, dtype=jnp.int32)
    table = jnp.max(jnp.where(key[:, None] == entries[None, :], numbers[:, None], -1), axis=0)
    table = jnp.where(table < 0, EMPTY, table)
    live = jnp.arange(capacity, dtype=jnp.int32)[None, :] < slot_counts[0][:, None]
    lists = jnp.where(live, send_rows[0], -1).reshape(ROW_TILES, TILE)

    vmem = pl.BlockSpec(memory_space=pltpu.VMEM)
    smem = pl.BlockSpec(memory_space=pltpu.SMEM)
    hbm = pl.BlockSpec(memory_space=pl.ANY)
    dma = pltpu.SemaphoreType.DMA
    return pl.pallas_call(
        functools.partial(kernel, blocks),
        out_shape=jax.ShapeDtypeStruct((ROWS, WIDTH), BF16),
        in_specs=[smem, smem, vmem, hbm, hbm, hbm, hbm, hbm],
        out_specs=vmem,
        scratch_shapes=[
            pltpu.VMEM((EMPTY + 1, TILE, TILE), BF16),
            pltpu.VMEM((EMPTY + 1, TILE, TILE), F32),
            pltpu.VMEM((ROWS, ROWS), BF16),
            pltpu.VMEM((2 * WIDTH, 2 * WIDTH), BF16),
            pltpu.VMEM((2 * WIDTH, 2 * WIDTH), BF16),
            pltpu.VMEM((2, SLOTS_NEAR, ROWS, WIDTH), BF16),
            pltpu.VMEM((ROW_TILES, TILE, WIDTH), F32),
            pltpu.VMEM((2, ROWS, WIDTH), BF16),
            pltpu.VMEM((ROWS, ROWS), BF16),
            pltpu.VMEM((2, GROUPS, RING * 8, WIDTH), BF16),
            pltpu.VMEM((2, GROUPS, RING * 8, WIDTH), BF16),
            pltpu.VMEM((2, RING, GROUPS * 8, WIDTH), BF16),
            pltpu.VMEM((2, RING, GROUPS * 8, WIDTH), BF16),
            pltpu.VMEM((ROWS, WIDTH), BF16),
            dma((5,)),
            dma((2, 8)),
            dma((2, SLOTS_NEAR, CHUNKS)),
            dma((2,)),
            dma((2,)),
            dma((2,)),
            dma((2,)),
            dma,
            dma((CHUNKS,)),
        ],
        compiler_params=pltpu.CompilerParams(
            collective_id=0, has_side_effects=True, vmem_limit_bytes=56 * 1024 * 1024
        ),
    )(table, earlier, lists, features, tile_values, far_weight, weight_one, weight_two)


def solution(mesh):
    placed = (
        P("blk", "col"),
        P("blk", None, None),
        P(None, "blk"),
        P("blk", None, None),
        P("blk", None),
        P("blk", None),
        P(),
        P(),
    )
    return jax.shard_map(
        body, mesh=mesh, in_specs=placed, out_specs=P("blk", "col"), check_vma=False
    )
```

```python
import functools

import jax
import jax.numpy as jnp
from jax import lax
from jax.experimental import pallas as pl
from jax.experimental.pallas import tpu as pltpu
from jax.sharding import PartitionSpec as P

MESH = pl.DeviceIdType.MESH
BF16 = jnp.bfloat16
F32 = jnp.float32
TILE = 128
REACH = 4
SLOTS_NEAR = 2 * REACH + 1
ROW_TILES = 8
ROWS = 1024
WIDTH = 128
CHUNKS = 4
CHUNK = ROWS // CHUNKS
RING = 16
GROUPS = 8
EMPTY = 288


def dot(a, b):
    return jnp.dot(a, b, preferred_element_type=F32)


def kernel(
    blocks, index_ref, lists_ref, counts_ref, x_hbm, tiles_hbm, far_hbm, w1_hbm, w2_hbm, out_ref,
    keys, plan_vmem, plan, tiles, sums, far, w1, w2, field, total, pair, picks, outgoing, middle, sorted_out, landed, arrived,
    load_sem, near_send, near_recv, group_send, group_recv, ring_send, ring_recv, col_send, col_recv,
):
    blk = lax.axis_index("blk")
    col = lax.axis_index("col")
    core = lax.rem(blk, 2)
    up = lax.rem(blk + 2, blocks)
    down = lax.rem(blk + blocks - 2, blocks)
    sibling = blk + 1 - 2 * core
    place = lax.rem(blk, RING)
    ring_base = blk - place
    group = blk // RING
    height = place // 2

    x_load = pltpu.make_async_copy(x_hbm, field.at[0, 4], load_sem.at[0])
    tiles_load = pltpu.make_async_copy(tiles_hbm, tiles.at[pl.ds(0, EMPTY)], load_sem.at[1])
    w1_load = pltpu.make_async_copy(w1_hbm, w1, load_sem.at[2])
    w2_load = pltpu.make_async_copy(w2_hbm, w2, load_sem.at[3])
    far_load = pltpu.make_async_copy(far_hbm, far, load_sem.at[4])
    x_load.start()
    tiles_load.start()
    far_load.start()
    w1_load.start()
    w2_load.start()

    barrier = pltpu.get_barrier_semaphore()

    def greet(**device):
        pl.semaphore_signal(barrier, inc=1, device_id=device, device_id_type=MESH)

    for k in range(1, RING):
        greet(blk=ring_base + lax.rem(place + k, RING))
    for k in range(1, GROUPS):
        greet(blk=lax.rem(group + k, GROUPS) * RING + place)
    greet(blk=up)
    greet(blk=down)
    greet(col=1 - col)

    def remote(src, dst, send, recv, **device):
        return pltpu.make_async_remote_copy(
            src_ref=src, dst_ref=dst, send_sem=send, recv_sem=recv, device_id=device, device_id_type=MESH
        )

    offset = index_ref[0:1, :] - blk + REACH
    offset = jnp.where(offset < 0, offset + blocks, offset)
    offset = jnp.where(offset >= blocks, offset - blocks, offset)
    keys[...] = jnp.full(keys.shape, -1, jnp.int32)
    keys[0:1, 0:EMPTY] = offset * 64 + index_ref[2:3, :] * ROW_TILES + index_ref[1:2, :]
    across = lax.broadcasted_iota(jnp.int32, (TILE, TILE), 1)
    along = lax.broadcasted_iota(jnp.int32, (TILE, TILE), 0)
    rows = [jnp.broadcast_to(keys[0:1, b * TILE : (b + 1) * TILE], (TILE, TILE)) for b in range(3)]
    columns = [row.T for row in rows]

    def last(hits):
        best = None
        for b, hit in hits:
            found = jnp.max(jnp.where(hit, along + b * TILE, -1), axis=0, keepdims=True)
            best = found if best is None else jnp.maximum(best, found)
        return jnp.where(best < 0, EMPTY, best)

    for g in range(5):
        plan_vmem[g : g + 1, :] = last([(b, columns[b] == across + g * TILE) for b in range(3)])
    for g in range(3):
        plan_vmem[5 + g : 6 + g, :] = last(
            [
                (b, (columns[b] == rows[g]) & (along < across) if b == g else columns[b] == rows[g])
                for b in range(g + 1)
            ]
        )
    plan_load = pltpu.make_async_copy(plan_vmem, plan, load_sem.at[5])
    plan_load.start()

    live = lax.broadcasted_iota(jnp.int32, (8, TILE), 0) < counts_ref[...]
    lists = jnp.where(live, lists_ref[...], -1)
    eight = lax.broadcasted_iota(jnp.int32, (8, TILE), 1)

    def mark(a, carry):
        turned = pltpu.roll(lists, lax.rem(TILE - 16 * a, TILE), 1)
        for k in range(0, 16, 2):
            first = jnp.broadcast_to(turned[:, k : k + 1], (8, TILE))
            second = jnp.broadcast_to(turned[:, k + 1 : k + 2], (8, TILE))
            for b in range(ROW_TILES):
                numbers = eight + b * TILE
                pairs = jnp.concatenate(
                    [jnp.where(first == numbers, 1.0, 0.0), jnp.where(second == numbers, 1.0, 0.0)], axis=0
                )
                start = pl.multiple_of(a * TILE + k * 8, 16)
                picks[pl.ds(start, 16), b * TILE : (b + 1) * TILE] = pairs.astype(BF16)
        return carry

    lax.fori_loop(0, ROW_TILES, mark, 0)

    def pick(layer):
        for a in range(CHUNKS):
            rows = dot(picks[a * CHUNK : (a + 1) * CHUNK, :], field[layer, 4])
            outgoing[layer, 2 * a : 2 * a + 2] = rows.astype(BF16).reshape(2, TILE, WIDTH)
        middle[layer, group] = outgoing[layer, group]

    def send_groups(layer):
        for k in range(1, GROUPS):
            other = lax.rem(group + k, GROUPS)
            remote(
                outgoing.at[layer, other], middle.at[layer, group],
                group_send.at[layer], group_recv.at[layer], blk=other * RING + place,
            ).start()

    def send_ring(layer):
        part = pl.ds(0, GROUPS - 1)
        remote(
            outgoing.at[layer, part], middle.at[layer, part], group_send.at[layer], group_recv.at[layer], blk=sibling
        ).wait_recv()
        rows = middle[layer].astype(F32).reshape(GROUPS, RING, 8, WIDTH)
        sorted_out[layer] = rows.transpose(1, 0, 2, 3).reshape(RING, GROUPS * 8, WIDTH).astype(BF16)
        landed[layer, place] = sorted_out[layer, place]
        for k in range(1, RING):
            other = lax.rem(place + k, RING)
            remote(
                sorted_out.at[layer, other], landed.at[layer, place],
                ring_send.at[layer], ring_recv.at[layer], blk=ring_base + other,
            ).start()

    def collect(layer):
        part = pl.ds(0, RING - 1)
        remote(
            sorted_out.at[layer, part], landed.at[layer, part], ring_send.at[layer], ring_recv.at[layer], blk=sibling
        ).wait_recv()
        rows = landed[layer].astype(F32).reshape(RING, GROUPS, 8, WIDTH)
        arrived[...] = rows.transpose(1, 0, 2, 3).reshape(ROWS, WIDTH).astype(BF16)

    def chunk(j):
        return pl.ds(pl.multiple_of(j * CHUNK, CHUNK), CHUNK)

    def send_near(layer, kind, j, source, target, device):
        remote(
            field.at[layer, source, chunk(j)], field.at[layer, target, chunk(j)],
            near_send.at[layer, kind], near_recv.at[layer, target, j], blk=device,
        ).start()

    def send_own(layer, j):
        send_near(layer, 0, j, 4, 2, up)
        send_near(layer, 1, j, 4, 6, down)
        send_near(layer, 2, j, 4, 3 + 2 * core, sibling)

    def wait_near(layer, slot, j):
        remote(
            field.at[layer, slot, chunk(j)], field.at[layer, slot, chunk(j)],
            near_send.at[layer, 0], near_recv.at[layer, slot, j], blk=sibling,
        ).wait_recv()

    def add(layer, terms, fresh=False):
        for r in range(0, ROW_TILES, 2):
            result = None if fresh else jnp.concatenate([total[r], total[r + 1]], axis=0)
            for slot, j in terms:
                values = jnp.concatenate(
                    [
                        jnp.concatenate(
                            [tiles[plan[slot // 2, slot % 2 * 64 + row * 8 + 2 * j + half]] for half in (0, 1)],
                            axis=1,
                        )
                        for row in (r, r + 1)
                    ],
                    axis=0,
                )
                product = dot(values, field[layer, slot, chunk(j)])
                result = product if result is None else result + product
            total[r] = result[:TILE]
            total[r + 1] = result[TILE:]

    own_odd, low_odd, high_odd, last_odd = 5 - 2 * core, 3 - 2 * core, 7 - 2 * core, 1 + 6 * core

    def aggregate(layer):
        add(layer, [(4, j) for j in range(CHUNKS)], fresh=True)

        def first_hop(j, carry):
            wait_near(layer, 2, j)
            send_near(layer, 3, j, 2, 0, up)
            send_near(layer, 4, j, 2, 1 + 2 * core, sibling)
            wait_near(layer, 6, j)
            send_near(layer, 5, j, 6, 8, down)
            send_near(layer, 6, j, 6, 5 + 2 * core, sibling)
            wait_near(layer, own_odd, j)
            add(layer, [(own_odd, j), (2, j), (6, j)])
            return carry

        lax.fori_loop(0, CHUNKS, first_hop, 0)

        def second_hop(j, carry):
            wait_near(layer, 0, j)
            wait_near(layer, 8, j)
            send_near(layer, 7, j, 8 - 8 * core, 7 - 6 * core, sibling)
            wait_near(layer, low_odd, j)
            wait_near(layer, high_odd, j)
            add(layer, [(0, j), (8, j), (low_odd, j), (high_odd, j)])
            return carry

        lax.fori_loop(0, CHUNKS // 2, second_hop, 0)
        send_ring(layer)
        lax.fori_loop(CHUNKS // 2, CHUNKS, second_hop, 0)

        def last_hop(j, carry):
            wait_near(layer, last_odd, j)
            return carry

        lax.fori_loop(0, CHUNKS, last_hop, 0)
        add(layer, [(last_odd, j) for j in range(CHUNKS)])
        collect(layer)

    def finish(j):
        near = jnp.concatenate([total[2 * j], total[2 * j + 1]], axis=0)
        return (near + dot(far[chunk(j)], arrived[...])).astype(BF16)

    x_load.wait()
    pick(0)
    pl.semaphore_wait(barrier, (RING - 1) + (GROUPS - 1) + 3)
    for j in range(CHUNKS):
        send_own(0, j)
    send_groups(0)

    plan_load.wait()
    tiles_load.wait()
    sums[EMPTY] = jnp.zeros((TILE, TILE), F32)
    tiles[EMPTY] = jnp.zeros((TILE, TILE), BF16)

    def add_earlier(t, carry):
        value = tiles[t].astype(F32) + sums[plan[5 + t // TILE, t % TILE]]
        sums[t] = value
        tiles[t] = value.astype(BF16)
        return carry

    lax.fori_loop(0, EMPTY, add_earlier, 0, unroll=2)

    aggregate(0)
    far_load.wait()

    def exchange(j):
        return remote(pair.at[col, chunk(j)], pair.at[col, chunk(j)], col_send, col_recv.at[j], col=1 - col)

    def finish_first(j, carry):
        pair[col, chunk(j)] = finish(j)
        exchange(j).start()
        return carry

    lax.fori_loop(0, CHUNKS, finish_first, 0)
    w1_load.wait()
    w2_load.wait()
    half = pl.ds(pl.multiple_of(col * WIDTH, WIDTH), WIDTH)

    def project(j, carry):
        remote(
            pair.at[1 - col, chunk(j)], pair.at[1 - col, chunk(j)], col_send, col_recv.at[j], col=1 - col
        ).wait_recv()
        both = jnp.concatenate([pair[0, chunk(j)], pair[1, chunk(j)]], axis=1)
        hidden = jnp.maximum(dot(both, w1[...]), 0.0).astype(BF16)
        field[1, 4, chunk(j)] = dot(hidden, w2[:, half]).astype(BF16)
        send_near(1, 2, j, 4, 3 + 2 * core, sibling)

        @pl.when(height != GROUPS - 1)
        def _():
            send_near(1, 0, j, 4, 2, up)

        @pl.when(height != 0)
        def _():
            send_near(1, 1, j, 4, 6, down)

        return carry

    lax.fori_loop(0, CHUNKS, project, 0)

    @pl.when(height == GROUPS - 1)
    def _():
        for j in range(CHUNKS):
            send_near(1, 0, j, 4, 2, up)

    @pl.when(height == 0)
    def _():
        for j in range(CHUNKS):
            send_near(1, 1, j, 4, 6, down)

    pick(1)
    send_groups(1)
    aggregate(1)

    def finish_second(j, carry):
        out_ref[chunk(j)] = finish(j)
        return carry

    lax.fori_loop(0, CHUNKS, finish_second, 0)

    for layer in range(2):
        for kind in range(8):
            remote(
                field.at[layer, 4], field.at[layer, 4], near_send.at[layer, kind], near_recv.at[layer, 4, 0], blk=sibling
            ).wait_send()
        part = pl.ds(0, GROUPS - 1)
        remote(
            outgoing.at[layer, part], middle.at[layer, part], group_send.at[layer], group_recv.at[layer], blk=sibling
        ).wait_send()
        part = pl.ds(0, RING - 1)
        remote(
            sorted_out.at[layer, part], landed.at[layer, part], ring_send.at[layer], ring_recv.at[layer], blk=sibling
        ).wait_send()
    remote(pair.at[0], pair.at[0], col_send, col_recv.at[0], col=1 - col).wait_send()


def body(
    features, tile_values, tile_index, send_rows, slot_counts, far_weight, weight_one, weight_two
):
    blocks = lax.axis_size("blk")
    vmem = pl.BlockSpec(memory_space=pltpu.VMEM)
    hbm = pl.BlockSpec(memory_space=pl.ANY)
    dma = pltpu.SemaphoreType.DMA
    return pl.pallas_call(
        functools.partial(kernel, blocks),
        out_shape=pltpu.VMEM((ROWS, WIDTH), BF16),
        in_specs=[vmem, vmem, vmem, hbm, hbm, hbm, hbm, hbm],
        out_specs=vmem,
        scratch_shapes=[
            pltpu.VMEM((8, 3 * TILE), jnp.int32),
            pltpu.VMEM((8, TILE), jnp.int32),
            pltpu.SMEM((8, TILE), jnp.int32),
            pltpu.VMEM((EMPTY + 1, TILE, TILE), BF16),
            pltpu.VMEM((EMPTY + 1, TILE, TILE), F32),
            pltpu.VMEM((ROWS, ROWS), BF16),
            pltpu.VMEM((2 * WIDTH, 2 * WIDTH), BF16),
            pltpu.VMEM((2 * WIDTH, 2 * WIDTH), BF16),
            pltpu.VMEM((2, SLOTS_NEAR, ROWS, WIDTH), BF16),
            pltpu.VMEM((ROW_TILES, TILE, WIDTH), F32),
            pltpu.VMEM((2, ROWS, WIDTH), BF16),
            pltpu.VMEM((ROWS, ROWS), BF16),
            pltpu.VMEM((2, GROUPS, RING * 8, WIDTH), BF16),
            pltpu.VMEM((2, GROUPS, RING * 8, WIDTH), BF16),
            pltpu.VMEM((2, RING, GROUPS * 8, WIDTH), BF16),
            pltpu.VMEM((2, RING, GROUPS * 8, WIDTH), BF16),
            pltpu.VMEM((ROWS, WIDTH), BF16),
            dma((6,)),
            dma((2, 8)),
            dma((2, SLOTS_NEAR, CHUNKS)),
            dma((2,)),
            dma((2,)),
            dma((2,)),
            dma((2,)),
            dma,
            dma((CHUNKS,)),
        ],
        compiler_params=pltpu.CompilerParams(
            collective_id=0, has_side_effects=True, vmem_limit_bytes=56 * 1024 * 1024
        ),
    )(
        tile_index, jnp.swapaxes(send_rows, 1, 2)[0], slot_counts,
        features, tile_values, far_weight, weight_one, weight_two,
    )


def solution(mesh):
    placed = (
        P("blk", "col"),
        P("blk", None, None),
        P(None, "blk"),
        P("blk", None, None),
        P("blk", None),
        P("blk", None),
        P(),
        P(),
    )
    return jax.shard_map(
        body, mesh=mesh, in_specs=placed, out_specs=P("blk", "col"), check_vma=False
    )
```

```python
import functools

import jax
import jax.numpy as jnp
from jax import lax
from jax.experimental import pallas as pl
from jax.experimental.pallas import tpu as pltpu
from jax.sharding import PartitionSpec as P

MESH = pl.DeviceIdType.MESH
BF16 = jnp.bfloat16
F32 = jnp.float32
TILE = 128
REACH = 4
SLOTS_NEAR = 2 * REACH + 1
ROW_TILES = 8
ROWS = 1024
WIDTH = 128
CHUNKS = 4
CHUNK = ROWS // CHUNKS
RING = 16
GROUPS = 8
EMPTY = 288
RING_AFTER = (3, 2)


def dot(a, b):
    return jnp.dot(a, b, preferred_element_type=F32)


def kernel(
    blocks, index_ref, lists_ref, counts_ref, x_hbm, tiles_hbm, far_hbm, w1_hbm, w2_hbm, out_ref,
    keys, plan_vmem, plan, tiles, sums, far, w1, w2, field, total, pair, picks, outgoing, middle, sorted_out, landed, arrived,
    load_sem, near_send, near_recv, group_send, group_recv, ring_send, ring_recv, col_send, col_recv,
):
    blk = lax.axis_index("blk")
    col = lax.axis_index("col")
    core = lax.rem(blk, 2)
    up = lax.rem(blk + 2, blocks)
    down = lax.rem(blk + blocks - 2, blocks)
    sibling = blk + 1 - 2 * core
    place = lax.rem(blk, RING)
    ring_base = blk - place
    group = blk // RING
    height = place // 2

    x_load = pltpu.make_async_copy(x_hbm, field.at[0, 4], load_sem.at[0])
    tiles_load = pltpu.make_async_copy(tiles_hbm, tiles.at[pl.ds(0, EMPTY)], load_sem.at[1])
    w1_load = pltpu.make_async_copy(w1_hbm, w1, load_sem.at[2])
    w2_load = pltpu.make_async_copy(w2_hbm, w2, load_sem.at[3])
    far_load = pltpu.make_async_copy(far_hbm, far, load_sem.at[4])
    x_load.start()
    tiles_load.start()
    far_load.start()
    w1_load.start()
    w2_load.start()

    barrier = pltpu.get_barrier_semaphore()

    def greet(**device):
        pl.semaphore_signal(barrier, inc=1, device_id=device, device_id_type=MESH)

    for k in range(1, RING):
        greet(blk=ring_base + lax.rem(place + k, RING))
    for k in range(1, GROUPS):
        greet(blk=lax.rem(group + k, GROUPS) * RING + place)
    greet(blk=up)
    greet(blk=down)
    greet(col=1 - col)

    def remote(src, dst, send, recv, **device):
        return pltpu.make_async_remote_copy(
            src_ref=src, dst_ref=dst, send_sem=send, recv_sem=recv, device_id=device, device_id_type=MESH
        )

    offset = index_ref[0:1, :] - blk + REACH
    offset = jnp.where(offset < 0, offset + blocks, offset)
    offset = jnp.where(offset >= blocks, offset - blocks, offset)
    keys[...] = jnp.full(keys.shape, -1, jnp.int32)
    keys[0:1, 0:EMPTY] = offset * 64 + index_ref[2:3, :] * ROW_TILES + index_ref[1:2, :]
    across = lax.broadcasted_iota(jnp.int32, (TILE, TILE), 1)
    along = lax.broadcasted_iota(jnp.int32, (TILE, TILE), 0)
    rows = [jnp.broadcast_to(keys[0:1, b * TILE : (b + 1) * TILE], (TILE, TILE)) for b in range(3)]
    columns = [row.T for row in rows]

    def last(hits):
        best = None
        for b, hit in hits:
            found = jnp.max(jnp.where(hit, along + b * TILE, -1), axis=0, keepdims=True)
            best = found if best is None else jnp.maximum(best, found)
        return jnp.where(best < 0, EMPTY, best)

    for g in range(5):
        plan_vmem[g : g + 1, :] = last([(b, columns[b] == across + g * TILE) for b in range(3)])
    for g in range(3):
        plan_vmem[5 + g : 6 + g, :] = last(
            [
                (b, (columns[b] == rows[g]) & (along < across) if b == g else columns[b] == rows[g])
                for b in range(g + 1)
            ]
        )
    plan_load = pltpu.make_async_copy(plan_vmem, plan, load_sem.at[5])
    plan_load.start()

    live = lax.broadcasted_iota(jnp.int32, (8, TILE), 0) < counts_ref[...]
    lists = jnp.where(live, lists_ref[...], -1)
    eight = lax.broadcasted_iota(jnp.int32, (8, TILE), 1)

    def mark(a, carry):
        turned = pltpu.roll(lists, lax.rem(TILE - 16 * a, TILE), 1)
        for k in range(0, 16, 2):
            first = jnp.broadcast_to(turned[:, k : k + 1], (8, TILE))
            second = jnp.broadcast_to(turned[:, k + 1 : k + 2], (8, TILE))
            for b in range(ROW_TILES):
                numbers = eight + b * TILE
                pairs = jnp.concatenate(
                    [jnp.where(first == numbers, 1.0, 0.0), jnp.where(second == numbers, 1.0, 0.0)], axis=0
                )
                start = pl.multiple_of(a * TILE + k * 8, 16)
                picks[pl.ds(start, 16), b * TILE : (b + 1) * TILE] = pairs.astype(BF16)
        return carry

    lax.fori_loop(0, ROW_TILES, mark, 0)

    def pick(layer):
        for a in range(CHUNKS):
            rows = dot(picks[a * CHUNK : (a + 1) * CHUNK, :], field[layer, 4])
            outgoing[layer, 2 * a : 2 * a + 2] = rows.astype(BF16).reshape(2, TILE, WIDTH)
        middle[layer, group] = outgoing[layer, group]

    def send_groups(layer):
        for k in range(1, GROUPS):
            other = lax.rem(group + k, GROUPS)
            remote(
                outgoing.at[layer, other], middle.at[layer, group],
                group_send.at[layer], group_recv.at[layer], blk=other * RING + place,
            ).start()

    def send_ring(layer):
        part = pl.ds(0, GROUPS - 1)
        remote(
            outgoing.at[layer, part], middle.at[layer, part], group_send.at[layer], group_recv.at[layer], blk=sibling
        ).wait_recv()
        rows = middle[layer].astype(F32).reshape(GROUPS, RING, 8, WIDTH)
        sorted_out[layer] = rows.transpose(1, 0, 2, 3).reshape(RING, GROUPS * 8, WIDTH).astype(BF16)
        landed[layer, place] = sorted_out[layer, place]
        for k in range(1, RING):
            other = lax.rem(place + k, RING)
            remote(
                sorted_out.at[layer, other], landed.at[layer, place],
                ring_send.at[layer], ring_recv.at[layer], blk=ring_base + other,
            ).start()

    def collect(layer):
        part = pl.ds(0, RING - 1)
        remote(
            sorted_out.at[layer, part], landed.at[layer, part], ring_send.at[layer], ring_recv.at[layer], blk=sibling
        ).wait_recv()
        rows = landed[layer].astype(F32).reshape(RING, GROUPS, 8, WIDTH)
        arrived[...] = rows.transpose(1, 0, 2, 3).reshape(ROWS, WIDTH).astype(BF16)

    def chunk(j):
        return pl.ds(pl.multiple_of(j * CHUNK, CHUNK), CHUNK)

    def send_near(layer, kind, j, source, target, device):
        remote(
            field.at[layer, source, chunk(j)], field.at[layer, target, chunk(j)],
            near_send.at[layer, kind], near_recv.at[layer, target, j], blk=device,
        ).start()

    def send_own(layer, j):
        send_near(layer, 0, j, 4, 2, up)
        send_near(layer, 1, j, 4, 6, down)
        send_near(layer, 2, j, 4, 3 + 2 * core, sibling)

    def wait_near(layer, slot, j):
        remote(
            field.at[layer, slot, chunk(j)], field.at[layer, slot, chunk(j)],
            near_send.at[layer, 0], near_recv.at[layer, slot, j], blk=sibling,
        ).wait_recv()

    def add(layer, terms, fresh=False):
        for r in range(0, ROW_TILES, 2):
            result = None if fresh else jnp.concatenate([total[r], total[r + 1]], axis=0)
            for slot, j in terms:
                values = jnp.concatenate(
                    [
                        jnp.concatenate(
                            [tiles[plan[slot // 2, slot % 2 * 64 + row * 8 + 2 * j + half]] for half in (0, 1)],
                            axis=1,
                        )
                        for row in (r, r + 1)
                    ],
                    axis=0,
                )
                product = dot(values, field[layer, slot, chunk(j)])
                result = product if result is None else result + product
            total[r] = result[:TILE]
            total[r + 1] = result[TILE:]

    own_odd, low_odd, high_odd, last_odd = 5 - 2 * core, 3 - 2 * core, 7 - 2 * core, 1 + 6 * core

    def aggregate(layer):
        add(layer, [(4, j) for j in range(CHUNKS)], fresh=True)

        def first_hop(j, carry):
            wait_near(layer, 2, j)
            send_near(layer, 3, j, 2, 0, up)
            send_near(layer, 4, j, 2, 1 + 2 * core, sibling)
            wait_near(layer, 6, j)
            send_near(layer, 5, j, 6, 8, down)
            send_near(layer, 6, j, 6, 5 + 2 * core, sibling)
            wait_near(layer, own_odd, j)
            add(layer, [(own_odd, j), (2, j), (6, j)])
            return carry

        lax.fori_loop(0, CHUNKS, first_hop, 0)

        def second_hop(j, carry):
            wait_near(layer, 0, j)
            wait_near(layer, 8, j)
            send_near(layer, 7, j, 8 - 8 * core, 7 - 6 * core, sibling)
            wait_near(layer, low_odd, j)
            wait_near(layer, high_odd, j)
            add(layer, [(0, j), (8, j), (low_odd, j), (high_odd, j)])
            return carry

        lax.fori_loop(0, RING_AFTER[layer], second_hop, 0)
        send_ring(layer)
        lax.fori_loop(RING_AFTER[layer], CHUNKS, second_hop, 0)

        def last_hop(j, carry):
            wait_near(layer, last_odd, j)
            add(layer, [(last_odd, j)])
            return carry

        lax.fori_loop(0, CHUNKS, last_hop, 0)
        collect(layer)

    def finish(j):
        near = jnp.concatenate([total[2 * j], total[2 * j + 1]], axis=0)
        return (near + dot(far[chunk(j)], arrived[...])).astype(BF16)

    x_load.wait()
    pick(0)
    pl.semaphore_wait(barrier, (RING - 1) + (GROUPS - 1) + 3)
    for j in range(CHUNKS):
        send_own(0, j)
    send_groups(0)

    plan_load.wait()
    tiles_load.wait()
    sums[EMPTY] = jnp.zeros((TILE, TILE), F32)
    tiles[EMPTY] = jnp.zeros((TILE, TILE), BF16)

    def add_earlier(t, carry):
        value = tiles[t].astype(F32) + sums[plan[5 + t // TILE, t % TILE]]
        sums[t] = value
        tiles[t] = value.astype(BF16)
        return carry

    lax.fori_loop(0, EMPTY, add_earlier, 0, unroll=2)

    aggregate(0)
    far_load.wait()

    def exchange(j):
        return remote(pair.at[col, chunk(j)], pair.at[col, chunk(j)], col_send, col_recv.at[j], col=1 - col)

    def finish_first(j, carry):
        pair[col, chunk(j)] = finish(j)
        exchange(j).start()
        return carry

    for j in range(CHUNKS):
        finish_first(j, 0)
    w1_load.wait()
    w2_load.wait()
    half = pl.ds(pl.multiple_of(col * WIDTH, WIDTH), WIDTH)

    def project(j, carry):
        remote(
            pair.at[1 - col, chunk(j)], pair.at[1 - col, chunk(j)], col_send, col_recv.at[j], col=1 - col
        ).wait_recv()
        both = jnp.concatenate([pair[0, chunk(j)], pair[1, chunk(j)]], axis=1)
        hidden = jnp.maximum(dot(both, w1[...]), 0.0).astype(BF16)
        field[1, 4, chunk(j)] = dot(hidden, w2[:, half]).astype(BF16)
        send_near(1, 2, j, 4, 3 + 2 * core, sibling)

        @pl.when(height != GROUPS - 1)
        def _():
            send_near(1, 0, j, 4, 2, up)

        @pl.when(height != 0)
        def _():
            send_near(1, 1, j, 4, 6, down)

        return carry

    lax.fori_loop(0, CHUNKS, project, 0)

    @pl.when(height == GROUPS - 1)
    def _():
        for j in range(CHUNKS):
            send_near(1, 0, j, 4, 2, up)

    @pl.when(height == 0)
    def _():
        for j in range(CHUNKS):
            send_near(1, 1, j, 4, 6, down)

    pick(1)
    send_groups(1)
    aggregate(1)

    def finish_second(j, carry):
        out_ref[chunk(j)] = finish(j)
        return carry

    for j in range(CHUNKS):
        finish_second(j, 0)

    for layer in range(2):
        for kind in range(8):
            remote(
                field.at[layer, 4], field.at[layer, 4], near_send.at[layer, kind], near_recv.at[layer, 4, 0], blk=sibling
            ).wait_send()
        part = pl.ds(0, GROUPS - 1)
        remote(
            outgoing.at[layer, part], middle.at[layer, part], group_send.at[layer], group_recv.at[layer], blk=sibling
        ).wait_send()
        part = pl.ds(0, RING - 1)
        remote(
            sorted_out.at[layer, part], landed.at[layer, part], ring_send.at[layer], ring_recv.at[layer], blk=sibling
        ).wait_send()
    remote(pair.at[0], pair.at[0], col_send, col_recv.at[0], col=1 - col).wait_send()


def body(
    features, tile_values, tile_index, send_rows, slot_counts, far_weight, weight_one, weight_two
):
    blocks = lax.axis_size("blk")
    vmem = pl.BlockSpec(memory_space=pltpu.VMEM)
    hbm = pl.BlockSpec(memory_space=pl.ANY)
    dma = pltpu.SemaphoreType.DMA
    return pl.pallas_call(
        functools.partial(kernel, blocks),
        out_shape=pltpu.VMEM((ROWS, WIDTH), BF16),
        in_specs=[vmem, vmem, vmem, hbm, hbm, hbm, hbm, hbm],
        out_specs=vmem,
        scratch_shapes=[
            pltpu.VMEM((8, 3 * TILE), jnp.int32),
            pltpu.VMEM((8, TILE), jnp.int32),
            pltpu.SMEM((8, TILE), jnp.int32),
            pltpu.VMEM((EMPTY + 1, TILE, TILE), BF16),
            pltpu.VMEM((EMPTY + 1, TILE, TILE), F32),
            pltpu.VMEM((ROWS, ROWS), BF16),
            pltpu.VMEM((2 * WIDTH, 2 * WIDTH), BF16),
            pltpu.VMEM((2 * WIDTH, 2 * WIDTH), BF16),
            pltpu.VMEM((2, SLOTS_NEAR, ROWS, WIDTH), BF16),
            pltpu.VMEM((ROW_TILES, TILE, WIDTH), F32),
            pltpu.VMEM((2, ROWS, WIDTH), BF16),
            pltpu.VMEM((ROWS, ROWS), BF16),
            pltpu.VMEM((2, GROUPS, RING * 8, WIDTH), BF16),
            pltpu.VMEM((2, GROUPS, RING * 8, WIDTH), BF16),
            pltpu.VMEM((2, RING, GROUPS * 8, WIDTH), BF16),
            pltpu.VMEM((2, RING, GROUPS * 8, WIDTH), BF16),
            pltpu.VMEM((ROWS, WIDTH), BF16),
            dma((6,)),
            dma((2, 8)),
            dma((2, SLOTS_NEAR, CHUNKS)),
            dma((2,)),
            dma((2,)),
            dma((2,)),
            dma((2,)),
            dma,
            dma((CHUNKS,)),
        ],
        compiler_params=pltpu.CompilerParams(
            collective_id=0, has_side_effects=True, vmem_limit_bytes=56 * 1024 * 1024
        ),
    )(
        tile_index, jnp.swapaxes(send_rows, 1, 2)[0], slot_counts,
        features, tile_values, far_weight, weight_one, weight_two,
    )


def solution(mesh):
    placed = (
        P("blk", "col"),
        P("blk", None, None),
        P(None, "blk"),
        P("blk", None, None),
        P("blk", None),
        P("blk", None),
        P(),
        P(),
    )
    return jax.shard_map(
        body, mesh=mesh, in_specs=placed, out_specs=P("blk", "col"), check_vma=False
    )
```
